32 devices in a mesh: tok: 4 (over y, x), ch: 8 (over z, core).
Axes of the slice: x: 2, y: 2, z: 4, core: 2. Of those that a mesh axis runs over, the one named last changes fastest.
Arguments:
- tokens: bfloat16 [64, 16384], P('tok', 'ch'), may hold values from -64 to 64
- probe: int32 [64, 16384], P('tok', 'ch'), may hold values from 0 to 1
- signs: int32 [16384], P('ch'), may hold values from 0 to 1
- gate_weight: bfloat16 [16384, 26624], P('ch', 'tok'), may hold values from -0.046875 to 0.046875
- up_weight: bfloat16 [16384, 26624], P('ch', 'tok'), may hold values from -0.046875 to 0.046875
- down_weight: bfloat16 [26624, 16384], P('tok', 'ch'), may hold values from -0.0390625 to 0.0390625
Outputs:
- rotated_product: float32 [64, 16384], P('tok', 'ch')
- diagonal_estimate: float32 [16384], P('ch')
The draws below stay inside these ranges and needn't reach their ends.
All inputs are finite; a program needn't handle non-finite values.
Results may differ from the reference program's by a relative error of at most 0.004.
Values may be sent and summed in bfloat16 or wider, within the bound.
A program may use at most 192 MiB of HBM per device.

```python
import math
import jax
import jax.numpy as jnp
from jax import lax

D = 16384
FF = 26624
TOKENS = 64


def draw_tokens(key, part):
    base_key, row_key, column_key = jax.random.split(key, 3)
    position = jnp.arange(TOKENS, dtype=jnp.float32) / max(TOKENS - 1, 1)
    row_factor = jnp.exp(jax.random.uniform(row_key, (TOKENS,), jnp.float32, math.log(0.6), math.log(1.5)))
    column_factor = jnp.exp(jax.random.uniform(column_key, (D,), jnp.float32, math.log(0.75), math.log(1.3)))
    values = jnp.clip(jax.random.normal(base_key, (TOKENS, D), jnp.float32), -6.0, 6.0)
    row_trend = jnp.exp(math.log(1.75) * position)
    return (values * (row_trend * row_factor)[:, None] * column_factor[None, :]).astype(jnp.bfloat16)


def touch_ends(drawn, stream_key, low, largest):
    dims = drawn.shape
    index_at = [jax.random.randint(jax.random.fold_in(stream_key, axis), (), 0, dims[axis]) for axis in range(len(dims))]
    drawn = drawn.at[tuple(index_at)].set(low)
    longest = dims.index(max(dims))
    index_at[longest] = (index_at[longest] + 1) % dims[longest]
    return drawn.at[tuple(index_at)].set(largest)


def level_of(stream_key, extent, pieces, smallest, top_value):
    def one(dim, parts):
        heights = jax.random.uniform(jax.random.fold_in(jax.random.fold_in(stream_key, 6), dim), (parts,), jnp.float32, smallest / len(pieces), top_value / len(pieces))
        return jnp.repeat(jnp.exp(heights), extent[dim] // parts).reshape((-1,) + (1,) * (len(extent) - dim - 1))

    factor_of = one(*pieces[0])
    for cut in pieces[1:]:
        factor_of = factor_of * one(*cut)
    return factor_of


def normal_values(rng, dims, spread, reach, cuts=(), kind=jnp.bfloat16):
    values = spread * jax.random.normal(rng, dims, jnp.float32)
    if cuts:
        values = values * level_of(rng, dims, cuts, -0.22, 0.18)
    return jnp.clip(values, -reach, reach).astype(kind)


def setup_inputs(seed: int = 0) -> dict:
    key_list = jax.random.split(jax.random.key(seed), 7)
    tokens = draw_tokens(jax.random.fold_in(key_list[6], 71), 0)
    probe = touch_ends(jax.random.randint(key_list[1], (TOKENS, D), 0, 2), jax.random.fold_in(key_list[1], 1), 0, 1).astype(jnp.int32)
    signs = touch_ends(jax.random.randint(key_list[2], (D,), 0, 2), jax.random.fold_in(key_list[2], 1), 0, 1).astype(jnp.int32)
    gate_weight = normal_values(key_list[3], (D, FF), D ** -0.5, 0.046875, ((0, 8), (1, 4)))
    up_weight = normal_values(key_list[4], (D, FF), D ** -0.5, 0.046875, ((0, 8), (1, 4)))
    down_weight = normal_values(key_list[5], (FF, D), FF ** -0.5, 0.0390625, ((0, 4), (1, 8)))
    return {"tokens": tokens, "probe": probe, "signs": signs, "gate_weight": gate_weight, "up_weight": up_weight, "down_weight": down_weight}


def walsh_transform(values):
    row_total, length = values.shape
    for bit_pos in range(length.bit_length() - 1):
        span_width = 2 ** bit_pos
        blocks = values.reshape(row_total, length // (2 * span_width), 2, span_width)
        lower_half = blocks[:, :, 0]
        upper_half = blocks[:, :, 1]
        values = jnp.stack([lower_half + upper_half, lower_half - upper_half], axis=2).reshape(row_total, length)
    return values

def reference(tokens, probe, signs, gate_weight, up_weight, down_weight):
    probe_signs = (2 * probe - 1).astype(jnp.float32)
    channel_signs = (2 * signs - 1).astype(jnp.float32)
    root_scale = 1.0 / math.sqrt(D)
    tangent = (walsh_transform(probe_signs * channel_signs[None, :]) * root_scale).astype(jnp.bfloat16)
    gate_pre = jnp.dot(tokens, gate_weight, preferred_element_type=jnp.float32)
    up_pre = jnp.dot(tokens, up_weight, preferred_element_type=jnp.float32)
    gate_tan = jnp.dot(tangent, gate_weight, preferred_element_type=jnp.float32)
    up_tan = jnp.dot(tangent, up_weight, preferred_element_type=jnp.float32)
    sigmoid_gate = jax.nn.sigmoid(gate_pre)
    activated = gate_pre * sigmoid_gate
    slope_term = sigmoid_gate * (1.0 + gate_pre * (1.0 - sigmoid_gate))
    hidden_tan = (slope_term * gate_tan * up_pre + activated * up_tan).astype(jnp.bfloat16)
    out_tangent = jnp.dot(hidden_tan, down_weight, preferred_element_type=jnp.float32).astype(jnp.bfloat16)
    back_hidden = jnp.dot(out_tangent, down_weight.T, preferred_element_type=jnp.float32)
    back_gate = (back_hidden * up_pre * slope_term).astype(jnp.bfloat16)
    back_up = (back_hidden * activated).astype(jnp.bfloat16)
    back_tokens = jnp.dot(back_gate, gate_weight.T, preferred_element_type=jnp.float32) + jnp.dot(back_up, up_weight.T, preferred_element_type=jnp.float32)
    rotated_product = walsh_transform(back_tokens) * root_scale * channel_signs[None, :]
    diagonal_estimate = lax.optimization_barrier(jnp.sum(probe_signs * rotated_product, axis=0)) / TOKENS
    return (rotated_product, diagonal_estimate)
```

```python
import functools
import math

import jax
import jax.numpy as jnp
from jax import lax
from jax.experimental import pallas as pl
from jax.experimental.pallas import tpu as pltpu
from jax.sharding import PartitionSpec as P

D = 16384
VMEM_LIMIT = 63 * 1024 * 1024


def partner_2(value, axis, stride):
    mask = 2**stride
    pairs = [(source, source ^ mask) for source in range(lax.axis_size(axis))]
    return lax.ppermute(value, axis, pairs)


def local_rotation(values):
    rows, length = values.shape
    lane = 128
    index = jnp.arange(lane, dtype=jnp.int32)
    parity = lax.population_count(index[:, None] & index[None, :]) & 1
    inner = jnp.where(parity == 0, 1.0, -1.0).astype(jnp.float32)
    values = jnp.dot(
        values.reshape(rows * (length // lane), lane),
        inner,
        precision=lax.Precision.HIGHEST,
        preferred_element_type=jnp.float32,
    ).reshape(rows, length // lane, lane)
    span = 1
    while span < length // lane:
        pairs = values.reshape(rows, length // lane // (2 * span), 2, span, lane)
        low, high = pairs[:, :, 0], pairs[:, :, 1]
        values = jnp.stack([low + high, low - high], axis=2)
        span *= 2
    return values.reshape(rows, length)


def cross_pairs(values):
    my_index = lax.axis_index("ch")
    for bit_pos in range(lax.axis_size("ch").bit_length() - 1):
        partner = partner_2(values, "ch", bit_pos)
        upper_half = my_index >> bit_pos & 1 == 1
        values = jnp.where(upper_half, partner - values, values + partner)
    return values


def cross_section(values):
    return cross_pairs(values)


SLOTS = 3
NT = (((1,), (1,)), ((), ()))


def layer_kernel(dims, x_in, gate_hbm, up_hbm, down_hbm, out_ref, *scratch):
    shards, rows, zs, chunks, width = dims
    (
        x, gate_buf, up_buf, down_buf, sums, to_sib, from_sib, from_z, slope_up, active, hid,
        out_acc, o_send, o_recv, o_all, sums2, to_sib2, from_sib2, to_z2, from_z2, grads,
        in_acc, k_send, k_recv,
        gate_sem, up_sem, down_sem, x_ss, x_rs, os_ss, os_rs, og_ss, og_rs, k_ss, k_rs,
        a_ss, a_rs, b_ss, b_rs, d_ss, d_rs, s_ss, s_rs,
        a2_ss, a2_rs, b2_ss, b2_rs, d2_ss, d2_rs, s2_ss, s2_rs,
    ) = scratch
    tok = lax.axis_index("tok")
    ch = lax.axis_index("ch")
    z, core = ch // 2, ch % 2
    per = shards // 4
    quarter = per * rows
    last = zs - 1
    f32, bf16 = jnp.float32, jnp.bfloat16

    def loads(f):
        slot = lax.rem(f, SLOTS)
        cols = pl.ds(pl.multiple_of(f * width, width), width)
        return (
            pltpu.make_async_copy(gate_hbm.at[:, cols], gate_buf.at[slot], gate_sem.at[slot]),
            pltpu.make_async_copy(up_hbm.at[:, cols], up_buf.at[slot], up_sem.at[slot]),
        )

    def load_down(f):
        at = pl.ds(pl.multiple_of(f * width, width), width)
        return pltpu.make_async_copy(down_hbm.at[at, :], down_buf.at[f], down_sem.at[f])

    def remote(src, dst, ss, rs, t, c):
        return pltpu.make_async_remote_copy(
            src_ref=src, dst_ref=dst, send_sem=ss, recv_sem=rs,
            device_id=(t, c), device_id_type=pl.DeviceIdType.MESH,
        )

    for f in range(SLOTS):
        for copy in loads(f):
            copy.start()

    sib = z * 2 + 1 - core
    barrier = pltpu.get_barrier_semaphore()

    def greet(t, c):
        pl.semaphore_signal(
            barrier, inc=1, device_id=(t, c), device_id_type=pl.DeviceIdType.MESH
        )

    for d in range(1, shards):
        greet(lax.rem(tok + d, shards), ch)
    greet(tok, sib)
    pl.when(z > 0)(lambda: greet(tok, ch - 2))
    pl.when(z < last)(lambda: greet(tok, ch + 2))
    inner = jnp.logical_and(z > 0, z < last)
    pl.when(inner)(lambda: pl.semaphore_wait(barrier, shards + 2))
    pl.when(jnp.logical_not(inner))(lambda: pl.semaphore_wait(barrier, shards + 1))

    def place(s):
        owner = s // per
        side = lax.rem(owner % 2 + core, 2)
        return (side * 2 + owner // 2) * per + s % per

    def peers(make):
        return [make(d, lax.rem(tok + d, shards)) for d in range(1, shards)]

    mine = pl.ds(pl.multiple_of(place(tok) * 2 * rows, 2 * rows), 2 * rows)
    x[mine, :] = x_in[...]
    gathers = peers(
        lambda d, p: remote(x_in, x.at[mine, :], x_ss.at[d - 1], x_rs.at[d - 1], p, ch)
    )
    for copy in gathers:
        copy.start()
    for copy in gathers:
        copy.wait()

    def ends():
        for e in range(2):
            far = last - z if e == 0 else z
            near = z if e == 0 else last - z
            toward = ch - 2 if e == 0 else ch + 2
            away = ch + 2 if e == 0 else ch - 2
            yield e, far, near, toward, away

    def in_range(f):
        return jnp.logical_and(f >= 0, f < chunks)

    def when(*conditions):
        return pl.when(functools.reduce(jnp.logical_and, conditions))

    def line(i, chunk_at, part, add_sib, a_copy, recv, b_copy, finish, block, d_copy, s_copy):
        n1 = i - 1

        @pl.when(in_range(n1))
        def _():
            a_copy(chunk_at(n1)).wait_recv()
            add_sib(chunk_at(n1))

        for e, far, near, toward, away in ends():
            n2 = i - 1 - far

            @pl.when(in_range(n2))
            def _():
                f = chunk_at(n2)

                @pl.when(far > 0)
                def _():
                    b_copy(e, f, toward).wait_recv()
                    recv(e, f)

                @pl.when(near > 0)
                def _():
                    part(e, f)
                    b_copy(e, f, toward).start()

                @pl.when(near == 0)
                def _():
                    finish(e, f)
                    d_copy(e, f, away).start()
                    s_copy(e, f).start()

            n3 = i - 1 - last - near

            @when(in_range(n3), near > 0)
            def _():
                f = chunk_at(n3)
                d_copy(e, f, away).wait_recv()

                @pl.when(far > 0)
                def _():
                    d_copy(e, f, away).start()

                s_copy(e, f).start()

    def drain(a_copy, b_copy, d_copy, s_copy):
        def body(f, carry):
            a_copy(f).wait_send()
            for e, far, near, toward, away in ends():
                pl.when(near > 0)(lambda: b_copy(e, f, toward).wait_send())
                pl.when(far > 0)(lambda: d_copy(e, f, away).wait_send())
                s_copy(e, f).wait_send()
            return carry

        lax.fori_loop(0, chunks, body, 0)

    lag = 2 + 2 * last

    def block_of(e):
        return pl.ds(pl.multiple_of((e * 2 + core) * quarter, quarter), quarter)

    half = pl.ds(0, 2 * quarter)

    def a_copy(f):
        return remote(to_sib.at[f], from_sib.at[f], a_ss.at[f], a_rs.at[f], tok, sib)

    def b_copy(e, f, c):
        return remote(
            sums.at[f, e], from_z.at[f, e], b_ss.at[e, f], b_rs.at[e, f], tok, c
        )

    def d_copy(e, f, c):
        ref = hid.at[f, block_of(e), :]
        return remote(ref, ref, d_ss.at[e, f], d_rs.at[e, f], tok, c)

    def s_copy(e, f):
        ref = hid.at[f, block_of(e), :]
        return remote(ref, ref, s_ss.at[e, f], s_rs.at[e, f], tok, sib)

    def sib_recv(e, f):
        other = pl.ds(pl.multiple_of((e * 2 + 1 - core) * quarter, quarter), quarter)
        ref = hid.at[f, other, :]
        return remote(ref, ref, s_ss.at[e, f], s_rs.at[e, f], tok, sib)

    def add_sib(f):
        sums[f] += from_sib[f]

    def recv(e, f):
        sums[f, e] += from_z[f, e]

    def finish(e, f):
        for p in range(per):
            base = p * 2 * rows
            gate_pre = sums[f, e, base : base + rows, :width]
            up_pre = sums[f, e, base : base + rows, width:]
            gate_tan = sums[f, e, base + rows : base + 2 * rows, :width]
            up_tan = sums[f, e, base + rows : base + 2 * rows, width:]
            sig = jax.nn.sigmoid(gate_pre)
            act = gate_pre * sig
            slope = sig * (1.0 + gate_pre * (1.0 - sig))
            su = slope * up_pre
            slope_up[f, p * rows : (p + 1) * rows, :] = su
            active[f, p * rows : (p + 1) * rows, :] = act
            at = (e * 2 + core) * quarter + p * rows
            hid[f, pl.ds(pl.multiple_of(at, rows), rows), :] = (
                su * gate_tan + act * up_tan
            ).astype(bf16)

    out_acc[...] = jnp.zeros_like(out_acc)

    def forward(i, carry):
        @pl.when(i < chunks)
        def _():
            load_down(i).start()
            for copy in loads(i):
                copy.wait()
            slot = lax.rem(i, SLOTS)
            for n, buf in enumerate((gate_buf, up_buf)):
                part = jnp.dot(x[...], buf[slot], preferred_element_type=f32)
                cols = slice(n * width, (n + 1) * width)
                for e in range(2):
                    sums[i, e, :, cols] = part[e * 2 * quarter : (e + 1) * 2 * quarter]
                to_sib[i, 0, :, cols] = part[4 * quarter : 6 * quarter]
                to_sib[i, 1, :, cols] = part[6 * quarter :]
            a_copy(i).start()

            @pl.when(i + SLOTS < chunks)
            def _():
                for copy in loads(i + SLOTS):
                    copy.start()

        line(
            i, lambda n: n, lambda e, f: None, add_sib, a_copy, recv, b_copy, finish, None,
            d_copy, s_copy,
        )
        n4 = i - lag

        @pl.when(n4 >= 0)
        def _():
            for e in range(2):
                sib_recv(e, n4).wait_recv()
            load_down(n4).wait()
            out_acc[...] += jnp.dot(hid[n4], down_buf[n4], preferred_element_type=f32)

        return carry

    lax.fori_loop(0, chunks + lag, forward, 0)
    drain(a_copy, b_copy, d_copy, s_copy)

    def scatter(acc, send, recv, ss, rs):
        send[...] = acc[...].astype(bf16)

        def make(d, p):
            at = pl.ds(pl.multiple_of(p * rows, rows), rows)
            return remote(send.at[at, :], recv.at[d - 1], ss.at[d - 1], rs.at[d - 1], p, ch)

        copies = peers(make)
        for copy in copies:
            copy.start()
        total = acc[pl.ds(pl.multiple_of(tok * rows, rows), rows), :]
        for d, copy in enumerate(copies):
            copy.wait()
            total = total + recv[d].astype(f32)
        return total

    here = pl.ds(pl.multiple_of(place(tok) * rows, rows), rows)
    o_all[here, :] = scatter(out_acc, o_send, o_recv, os_ss, os_rs).astype(bf16)
    gathers = peers(
        lambda d, p: remote(
            o_all.at[here, :], o_all.at[here, :], og_ss.at[d - 1], og_rs.at[d - 1], p, ch
        )
    )
    for copy in gathers:
        copy.start()
    for d, copy in enumerate(gathers):
        copy.wait()

    def a2_copy(f):
        return remote(to_sib2.at[f], from_sib2.at[f], a2_ss.at[f], a2_rs.at[f], tok, sib)

    def b2_copy(e, f, c):
        return remote(
            to_z2.at[f, e], from_z2.at[f, e], b2_ss.at[e, f], b2_rs.at[e, f], tok, c
        )

    def d2_copy(e, f, c):
        ref = grads.at[f, e * 2 + core]
        return remote(ref, ref, d2_ss.at[e, f], d2_rs.at[e, f], tok, c)

    def s2_copy(e, f):
        ref = grads.at[f, e * 2 + core]
        return remote(ref, ref, s2_ss.at[e, f], s2_rs.at[e, f], tok, sib)

    def sib2_recv(e, f):
        ref = grads.at[f, e * 2 + 1 - core]
        return remote(ref, ref, s2_ss.at[e, f], s2_rs.at[e, f], tok, sib)

    def add_sib2(f):
        sums2[f] += from_sib2[f]

    def recv2(e, f):
        sums2[f, e] += from_z2[f, e].astype(f32)

    def part2(e, f):
        to_z2[f, e] = sums2[f, e].astype(bf16)

    def finish2(e, f):
        back = sums2[f, e]
        grads[f, e * 2 + core, 0] = (back * slope_up[f]).astype(bf16)
        grads[f, e * 2 + core, 1] = (back * active[f]).astype(bf16)

    def chunk_at(n):
        return chunks - 1 - n

    in_acc[...] = jnp.zeros_like(in_acc)

    def backward(i, carry):
        @pl.when(i < chunks)
        def _():
            f = chunk_at(i)
            part = lax.dot_general(o_all[...], down_buf[f], NT, preferred_element_type=f32)
            for e in range(2):
                sums2[f, e] = part[e * quarter : (e + 1) * quarter]
                to_sib2[f, e] = part[(2 + e) * quarter : (3 + e) * quarter]
            a2_copy(f).start()

        line(
            i, chunk_at, part2, add_sib2, a2_copy, recv2, b2_copy, finish2, None, d2_copy, s2_copy
        )
        n4 = i - lag

        @pl.when(n4 >= 0)
        def _():
            f = chunk_at(n4)
            for e in range(2):
                sib2_recv(e, f).wait_recv()

            @pl.when(f + SLOTS < chunks)
            def _():
                for copy in loads(f):
                    copy.wait()

            slot = lax.rem(f, SLOTS)
            both = grads[f]
            for n, buf in enumerate((gate_buf, up_buf)):
                piece = both[:, n].reshape(4 * quarter, width)
                in_acc[...] += lax.dot_general(piece, buf[slot], NT, preferred_element_type=f32)

            @pl.when(f >= SLOTS)
            def _():
                for copy in loads(f - SLOTS):
                    copy.start()

        return carry

    lax.fori_loop(0, chunks + lag, backward, 0)
    drain(a2_copy, b2_copy, d2_copy, s2_copy)
    out_ref[...] = scatter(in_acc, k_send, k_recv, k_ss, k_rs)


def layer(local, gate_weight, up_weight, down_weight):
    shards, ways = lax.axis_size("tok"), lax.axis_size("ch")
    rows, depth = local.shape[0] // 2, local.shape[1]
    hidden = gate_weight.shape[1]
    width = max(w for w in range(128, 513, 128) if hidden % w == 0)
    chunks = hidden // width
    total, quarter = shards * rows, shards * rows // 4
    dims = (shards, rows, ways // 2, chunks, width)
    f32, bf16, vmem = jnp.float32, jnp.bfloat16, pltpu.VMEM
    dma = pltpu.SemaphoreType.DMA
    scratch = [
        vmem((2 * total, depth), bf16),
        vmem((SLOTS, depth, width), bf16),
        vmem((SLOTS, depth, width), bf16),
        vmem((chunks, width, depth), bf16),
        vmem((chunks, 2, 2 * quarter, 2 * width), f32),
        vmem((chunks, 2, 2 * quarter, 2 * width), f32),
        vmem((chunks, 2, 2 * quarter, 2 * width), f32),
        vmem((chunks, 2, 2 * quarter, 2 * width), f32),
        vmem((chunks, quarter, width), f32),
        vmem((chunks, quarter, width), f32),
        vmem((chunks, total, width), bf16),
        vmem((total, depth), f32),
        vmem((total, depth), bf16),
        vmem((shards - 1, rows, depth), bf16),
        vmem((total, depth), bf16),
        vmem((chunks, 2, quarter, width), f32),
        vmem((chunks, 2, quarter, width), f32),
        vmem((chunks, 2, quarter, width), f32),
        vmem((chunks, 2, quarter, width), bf16),
        vmem((chunks, 2, quarter, width), bf16),
        vmem((chunks, 4, 2, quarter, width), bf16),
        vmem((total, depth), f32),
        vmem((total, depth), bf16),
        vmem((shards - 1, rows, depth), bf16),
        dma((SLOTS,)), dma((SLOTS,)), dma((chunks,)),
        *[dma((shards - 1,)) for _ in range(8)],
    ]
    for _ in range(2):
        scratch += [dma((chunks,)), dma((chunks,))]
        scratch += [dma((2, chunks)) for _ in range(6)]
    flops = 2 * total * depth * hidden * 8
    return pl.pallas_call(
        functools.partial(layer_kernel, dims),
        out_shape=jax.ShapeDtypeStruct((rows, depth), f32),
        in_specs=[pl.BlockSpec(memory_space=vmem)] + [pl.BlockSpec(memory_space=pl.ANY)] * 3,
        out_specs=pl.BlockSpec(memory_space=vmem),
        scratch_shapes=scratch,
        compiler_params=pltpu.CompilerParams(
            collective_id=0, has_side_effects=True, vmem_limit_bytes=VMEM_LIMIT
        ),
        cost_estimate=pl.CostEstimate(
            flops=flops, bytes_accessed=10 * depth * hidden, transcendentals=0
        ),
    )(local, gate_weight, up_weight, down_weight)


def on_device(tokens, probe, signs, gate_weight, up_weight, down_weight):
    tok_rows, channels = tokens.shape
    total_rows = tok_rows * lax.axis_size("tok")
    root_scale = 1.0 / math.sqrt(D)
    probe_signs = (2 * probe - 1).astype(jnp.float32)
    channel_signs = (2 * signs - 1).astype(jnp.float32)
    start_local = local_rotation(probe_signs * channel_signs[None, :])
    tangent = (cross_section(start_local) * root_scale).astype(jnp.bfloat16)
    back_tokens = layer(
        jnp.concatenate([tokens, tangent], axis=0), gate_weight, up_weight, down_weight
    )
    local_back = local_rotation(back_tokens)
    rotated_product = cross_section(local_back) * root_scale * channel_signs[None, :]
    token_terms = jnp.sum(probe_signs * rotated_product, axis=0)
    diagonal_estimate = lax.psum(token_terms, "tok") / total_rows
    return (rotated_product, diagonal_estimate)


def solution(mesh):
    placed = (
        P("tok", "ch"),
        P("tok", "ch"),
        P("ch"),
        P("ch", "tok"),
        P("ch", "tok"),
        P("tok", "ch"),
    )
    return jax.shard_map(
        on_device, mesh=mesh, in_specs=placed, out_specs=(P("tok", "ch"), P("ch")), check_vma=False
    )
```

```python
import functools
import math

import jax
import jax.numpy as jnp
from jax import lax
from jax.experimental import pallas as pl
from jax.experimental.pallas import tpu as pltpu
from jax.sharding import PartitionSpec as P

D = 16384
VMEM_LIMIT = 63 * 1024 * 1024


LANE = 128
SLOTS = 3
HOP = 2
NT = (((1,), (1,)), ((), ()))


def butterfly(parts):
    span = 1
    while span < len(parts):
        for n in range(len(parts)):
            if n & span == 0:
                low, high = parts[n], parts[n + span]
                parts[n], parts[n + span] = low + high, low - high
        span *= 2
    return parts


def rotate_local(values, inner, precision):
    rows, lane = values.shape[0], inner.shape[0]
    groups = values.shape[1] // lane
    stacked = jnp.concatenate([values[:, g * lane : (g + 1) * lane] for g in range(groups)], axis=0)
    turned = jnp.dot(stacked, inner, precision=precision, preferred_element_type=jnp.float32)
    parts = butterfly([turned[g * rows : (g + 1) * rows] for g in range(groups)])
    return jnp.concatenate(parts, axis=1)


def layer_kernel(
    dims, tokens_in, probe, signs, inner, gate_hbm, up_hbm, down_hbm, out_ref, diag_ref, *scratch
):
    shards, rows, ways, chunks, width, owners = dims
    zs = ways // 2
    (
        x, gate_buf, up_buf, down_buf, sums, to_sib, from_sib, from_z, slope_up, active, hid,
        out_acc, o_send, o_recv, o_all, sums2, to_sib2, from_sib2, to_z2, from_z2, grads,
        k_send, k_recv, x_in, t_own, t_got, t_sum, t_res, f_own, f_got, f_sum, f_res,
        diag_own, diag_got,
        gate_sem, up_sem, down_sem, x_ss, x_rs, os_ss, os_rs, og_ss, og_rs, k_ss, k_rs,
        a_ss, a_rs, b_ss, b_rs, d_ss, d_rs, s_ss, s_rs,
        a2_ss, a2_rs, b2_ss, b2_rs, d2_ss, d2_rs, s2_ss, s2_rs,
        t1_ss, t1_rs, t2_ss, t2_rs, f1_ss, f1_rs, f2_ss, f2_rs, g_ss, g_rs,
    ) = scratch
    in_acc = out_acc
    tok = lax.axis_index("tok")
    ch = lax.axis_index("ch")
    z, core = ch // 2, ch % 2
    per = shards // 4
    quarter = per * rows
    last = zs - 1
    f32, bf16 = jnp.float32, jnp.bfloat16

    def loads(f):
        slot = lax.rem(f, SLOTS)
        cols = pl.ds(pl.multiple_of(f * width, width), width)
        return (
            pltpu.make_async_copy(gate_hbm.at[:, cols], gate_buf.at[slot], gate_sem.at[slot]),
            pltpu.make_async_copy(up_hbm.at[:, cols], up_buf.at[slot], up_sem.at[slot]),
        )

    def load_down(f):
        at = pl.ds(pl.multiple_of(f * width, width), width)
        return pltpu.make_async_copy(down_hbm.at[at, :], down_buf.at[f], down_sem.at[f])

    def remote(src, dst, ss, rs, t, c):
        return pltpu.make_async_remote_copy(
            src_ref=src, dst_ref=dst, send_sem=ss, recv_sem=rs,
            device_id=(t, c), device_id_type=pl.DeviceIdType.MESH,
        )

    for f in range(SLOTS):
        for copy in loads(f):
            copy.start()

    sib = z * 2 + 1 - core
    barrier = pltpu.get_barrier_semaphore()

    def greet(t, c):
        pl.semaphore_signal(
            barrier, inc=1, device_id=(t, c), device_id_type=pl.DeviceIdType.MESH
        )

    for d in range(1, shards):
        greet(lax.rem(tok + d, shards), ch)
    for d in range(1, ways):
        greet(tok, lax.rem(ch + d, ways))
    pl.semaphore_wait(barrier, shards + ways - 2)

    def only(index, run):
        if owners == ways:
            run()
        else:
            pl.when(index < owners)(run)

    def across(own, got, summed, res, ss1, rs1, ss2, rs2):
        others = range(1, ways)
        to = {d: lax.rem(ch + d, ways) for d in others}
        of = {d: lax.rem(ch + ways - d, ways) for d in others}

        def out1(d):
            return remote(own.at[to[d]], got.at[ch], ss1.at[d], rs1.at[ch], tok, to[d])

        def in1(d):
            return remote(own.at[0], got.at[of[d]], ss1.at[d], rs1.at[of[d]], tok, of[d])

        def out2(d):
            return remote(summed.at[to[d]], res.at[ch], ss2.at[d], rs2.at[ch], tok, to[d])

        def in2(d):
            return remote(summed.at[0], res.at[of[d]], ss2.at[d], rs2.at[of[d]], tok, of[d])

        for d in others:
            only(to[d], lambda: out1(d).start())

        def combine():
            got[ch] = own[ch]
            for d in others:
                in1(d).wait_recv()
            parts = butterfly([got[n].astype(f32) for n in range(ways)])
            for n in range(ways):
                summed[n] = parts[n].astype(summed.dtype)
            for d in others:
                out2(d).start()
            res[ch] = summed[ch]

        only(ch, combine)
        for d in others:
            only(of[d], lambda: in2(d).wait_recv())
            only(to[d], lambda: out1(d).wait_send())
        only(ch, lambda: [out2(d).wait_send() for d in others] and None)

    root_scale = 1.0 / math.sqrt(D)
    piece = tokens_in.shape[1] // owners
    channel_signs = (2 * signs[...] - 1).astype(f32)
    probe_signs = (2 * probe[...] - 1).astype(f32)
    start = (probe_signs * channel_signs).astype(bf16)
    for n in range(owners):
        t_own[n] = start[:, n * piece : (n + 1) * piece]
    across(t_own, t_got, t_sum, t_res, t1_ss, t1_rs, t2_ss, t2_rs)
    start = jnp.concatenate([t_res[n] for n in range(owners)], axis=1)
    x_in[:rows] = tokens_in[...]
    x_in[rows:] = (rotate_local(start, inner[...], None) * root_scale).astype(bf16)

    def place(s):
        owner = s // per
        side = lax.rem(owner % 2 + core, 2)
        return (side * 2 + owner // 2) * per + s % per

    def peers(make):
        return [make(d, lax.rem(tok + d, shards)) for d in range(1, shards)]

    mine = pl.ds(pl.multiple_of(place(tok) * 2 * rows, 2 * rows), 2 * rows)
    x[mine, :] = x_in[...]
    gathers = peers(
        lambda d, p: remote(x_in, x.at[mine, :], x_ss.at[d - 1], x_rs.at[d - 1], p, ch)
    )
    for copy in gathers:
        copy.start()
    for copy in gathers:
        copy.wait()

    def ends():
        for e in range(2):
            far = last - z if e == 0 else z
            near = z if e == 0 else last - z
            toward = ch - 2 if e == 0 else ch + 2
            away = ch + 2 if e == 0 else ch - 2
            yield e, far, near, toward, away

    def in_range(f):
        return jnp.logical_and(f >= 0, f < chunks)

    def when(*conditions):
        return pl.when(functools.reduce(jnp.logical_and, conditions))

    def line(i, hop, chunk_at, part, add_sib, a_copy, recv, b_copy, finish, d_copy, s_copy):
        n1 = i - 1

        @pl.when(in_range(n1))
        def _():
            a_copy(chunk_at(n1)).wait_recv()
            add_sib(chunk_at(n1))

        for e, far, near, toward, away in ends():
            n2 = i - 1 - hop * far

            @pl.when(in_range(n2))
            def _():
                f = chunk_at(n2)

                @pl.when(far > 0)
                def _():
                    b_copy(e, f, toward).wait_recv()
                    recv(e, f)

                @pl.when(near > 0)
                def _():
                    part(e, f)
                    b_copy(e, f, toward).start()

                @pl.when(near == 0)
                def _():
                    finish(e, f)
                    d_copy(e, f, away).start()
                    s_copy(e, f).start()

            n3 = i - 1 - hop * last - near

            @when(in_range(n3), near > 0)
            def _():
                f = chunk_at(n3)
                d_copy(e, f, away).wait_recv()

                @pl.when(far > 0)
                def _():
                    d_copy(e, f, away).start()

                s_copy(e, f).start()

    def drain(a_copy, b_copy, d_copy, s_copy):
        def body(f, carry):
            a_copy(f).wait_send()
            for e, far, near, toward, away in ends():
                pl.when(near > 0)(lambda: b_copy(e, f, toward).wait_send())
                pl.when(far > 0)(lambda: d_copy(e, f, away).wait_send())
                s_copy(e, f).wait_send()
            return carry

        lax.fori_loop(0, chunks, body, 0)

    lag, lag2 = 2 + (1 + HOP) * last, 2 + 2 * last

    def block_of(e):
        return pl.ds(pl.multiple_of((e * 2 + core) * quarter, quarter), quarter)

    half = pl.ds(0, 2 * quarter)

    def a_copy(f):
        return remote(to_sib.at[f], from_sib.at[f], a_ss.at[f], a_rs.at[f], tok, sib)

    def b_copy(e, f, c):
        return remote(
            sums.at[f, e], from_z.at[f, e], b_ss.at[e, f], b_rs.at[e, f], tok, c
        )

    def d_copy(e, f, c):
        ref = hid.at[f, block_of(e), :]
        return remote(ref, ref, d_ss.at[e, f], d_rs.at[e, f], tok, c)

    def s_copy(e, f):
        ref = hid.at[f, block_of(e), :]
        return remote(ref, ref, s_ss.at[e, f], s_rs.at[e, f], tok, sib)

    def sib_recv(e, f):
        other = pl.ds(pl.multiple_of((e * 2 + 1 - core) * quarter, quarter), quarter)
        ref = hid.at[f, other, :]
        return remote(ref, ref, s_ss.at[e, f], s_rs.at[e, f], tok, sib)

    def add_sib(f):
        sums[f] += from_sib[f]

    def recv(e, f):
        sums[f, e] += from_z[f, e]

    def finish(e, f):
        for p in range(per):
            base = p * 2 * rows
            gate_pre = sums[f, e, base : base + rows, :width]
            up_pre = sums[f, e, base : base + rows, width:]
            gate_tan = sums[f, e, base + rows : base + 2 * rows, :width]
            up_tan = sums[f, e, base + rows : base + 2 * rows, width:]
            sig = jax.nn.sigmoid(gate_pre)
            act = gate_pre * sig
            slope = sig * (1.0 + gate_pre * (1.0 - sig))
            su = slope * up_pre
            slope_up[f, p * rows : (p + 1) * rows, :] = su
            active[f, p * rows : (p + 1) * rows, :] = act
            at = (e * 2 + core) * quarter + p * rows
            hid[f, pl.ds(pl.multiple_of(at, rows), rows), :] = (
                su * gate_tan + act * up_tan
            ).astype(bf16)

    out_acc[...] = jnp.zeros_like(out_acc)

    def forward(i, carry):
        @pl.when(i < chunks)
        def _():
            load_down(i).start()
            for copy in loads(i):
                copy.wait()
            slot = lax.rem(i, SLOTS)
            for n, buf in enumerate((gate_buf, up_buf)):
                part = jnp.dot(x[...], buf[slot], preferred_element_type=f32)
                cols = slice(n * width, (n + 1) * width)
                for e in range(2):
                    sums[i, e, :, cols] = part[e * 2 * quarter : (e + 1) * 2 * quarter]
                to_sib[i, 0, :, cols] = part[4 * quarter : 6 * quarter]
                to_sib[i, 1, :, cols] = part[6 * quarter :]
            a_copy(i).start()

            @pl.when(i + SLOTS < chunks)
            def _():
                for copy in loads(i + SLOTS):
                    copy.start()

        line(
            i, HOP, lambda n: n, lambda e, f: None, add_sib, a_copy, recv, b_copy, finish,
            d_copy, s_copy,
        )
        n4 = i - lag

        @pl.when(n4 >= 0)
        def _():
            for e in range(2):
                sib_recv(e, n4).wait_recv()
            load_down(n4).wait()
            out_acc[...] += jnp.dot(hid[n4], down_buf[n4], preferred_element_type=f32)

        return carry

    lax.fori_loop(0, chunks + lag, forward, 0)
    drain(a_copy, b_copy, d_copy, s_copy)

    def scatter(acc, send, recv, ss, rs):
        send[...] = acc[...].astype(bf16)

        def make(d, p):
            at = pl.ds(pl.multiple_of(p * rows, rows), rows)
            return remote(send.at[at, :], recv.at[d - 1], ss.at[d - 1], rs.at[d - 1], p, ch)

        copies = peers(make)
        for copy in copies:
            copy.start()
        total = acc[pl.ds(pl.multiple_of(tok * rows, rows), rows), :]
        for d, copy in enumerate(copies):
            copy.wait()
            total = total + recv[d].astype(f32)
        return total

    here = pl.ds(pl.multiple_of(place(tok) * rows, rows), rows)
    o_all[here, :] = scatter(out_acc, o_send, o_recv, os_ss, os_rs).astype(bf16)
    gathers = peers(
        lambda d, p: remote(
            o_all.at[here, :], o_all.at[here, :], og_ss.at[d - 1], og_rs.at[d - 1], p, ch
        )
    )
    for copy in gathers:
        copy.start()
    for d, copy in enumerate(gathers):
        copy.wait()

    def a2_copy(f):
        return remote(to_sib2.at[f], from_sib2.at[f], a2_ss.at[f], a2_rs.at[f], tok, sib)

    def b2_copy(e, f, c):
        return remote(
            to_z2.at[f, e], from_z2.at[f, e], b2_ss.at[e, f], b2_rs.at[e, f], tok, c
        )

    def d2_copy(e, f, c):
        ref = grads.at[f, e * 2 + core]
        return remote(ref, ref, d2_ss.at[e, f], d2_rs.at[e, f], tok, c)

    def s2_copy(e, f):
        ref = grads.at[f, e * 2 + core]
        return remote(ref, ref, s2_ss.at[e, f], s2_rs.at[e, f], tok, sib)

    def sib2_recv(e, f):
        ref = grads.at[f, e * 2 + 1 - core]
        return remote(ref, ref, s2_ss.at[e, f], s2_rs.at[e, f], tok, sib)

    def add_sib2(f):
        sums2[f] += from_sib2[f]

    def recv2(e, f):
        sums2[f, e] += from_z2[f, e].astype(f32)

    def part2(e, f):
        to_z2[f, e] = sums2[f, e].astype(bf16)

    def finish2(e, f):
        back = sums2[f, e]
        grads[f, e * 2 + core, 0] = (back * slope_up[f]).astype(bf16)
        grads[f, e * 2 + core, 1] = (back * active[f]).astype(bf16)

    def chunk_at(n):
        return chunks - 1 - n

    in_acc[...] = jnp.zeros_like(in_acc)

    def backward(i, carry):
        @pl.when(i < chunks)
        def _():
            f = chunk_at(i)
            part = lax.dot_general(o_all[...], down_buf[f], NT, preferred_element_type=f32)
            for e in range(2):
                sums2[f, e] = part[e * quarter : (e + 1) * quarter]
                to_sib2[f, e] = part[(2 + e) * quarter : (3 + e) * quarter]
            a2_copy(f).start()

        line(
            i, 1, chunk_at, part2, add_sib2, a2_copy, recv2, b2_copy, finish2, d2_copy, s2_copy
        )
        n4 = i - lag2

        @pl.when(n4 >= 0)
        def _():
            f = chunk_at(n4)
            for e in range(2):
                sib2_recv(e, f).wait_recv()

            @pl.when(f + SLOTS < chunks)
            def _():
                for copy in loads(f):
                    copy.wait()

            slot = lax.rem(f, SLOTS)
            both = grads[f]
            for n, buf in enumerate((gate_buf, up_buf)):
                piece = both[:, n].reshape(4 * quarter, width)
                in_acc[...] += lax.dot_general(piece, buf[slot], NT, preferred_element_type=f32)

            @pl.when(f >= SLOTS)
            def _():
                for copy in loads(f - SLOTS):
                    copy.start()

        return carry

    lax.fori_loop(0, chunks + lag2, backward, 0)
    drain(a2_copy, b2_copy, d2_copy, s2_copy)
    back_tokens = scatter(in_acc, k_send, k_recv, k_ss, k_rs)
    turned = rotate_local(back_tokens, inner[...].astype(f32), lax.Precision.HIGHEST)
    for n in range(owners):
        f_own[n] = turned[:, n * piece : (n + 1) * piece]
    across(f_own, f_got, f_sum, f_res, f1_ss, f1_rs, f2_ss, f2_rs)
    turned = jnp.concatenate([f_res[n] for n in range(owners)], axis=1)
    product = turned * root_scale * channel_signs
    out_ref[...] = product
    diag_own[...] = jnp.sum(probe_signs * product, axis=0, keepdims=True)
    copies = peers(
        lambda d, p: remote(diag_own, diag_got.at[d - 1], g_ss.at[d - 1], g_rs.at[d - 1], p, ch)
    )
    for copy in copies:
        copy.start()
    diagonal = diag_own[...]
    for d, copy in enumerate(copies):
        copy.wait()
        diagonal = diagonal + diag_got[d]
    diag_ref[...] = diagonal / (shards * rows)


def layer(tokens, probe, signs, inner, gate_weight, up_weight, down_weight):
    shards, ways = lax.axis_size("tok"), lax.axis_size("ch")
    rows, depth = tokens.shape
    hidden = gate_weight.shape[1]
    width = max(w for w in range(128, 513, 128) if hidden % w == 0)
    chunks = hidden // width
    total, quarter = shards * rows, shards * rows // 4
    owners = min(ways, depth // LANE)
    piece = depth // owners
    dims = (shards, rows, ways, chunks, width, owners)
    f32, bf16, vmem = jnp.float32, jnp.bfloat16, pltpu.VMEM
    dma = pltpu.SemaphoreType.DMA
    scratch = [
        vmem((2 * total, depth), bf16),
        vmem((SLOTS, depth, width), bf16),
        vmem((SLOTS, depth, width), bf16),
        vmem((chunks, width, depth), bf16),
        vmem((chunks, 2, 2 * quarter, 2 * width), f32),
        vmem((chunks, 2, 2 * quarter, 2 * width), f32),
        vmem((chunks, 2, 2 * quarter, 2 * width), f32),
        vmem((chunks, 2, 2 * quarter, 2 * width), f32),
        vmem((chunks, quarter, width), f32),
        vmem((chunks, quarter, width), f32),
        vmem((chunks, total, width), bf16),
        vmem((total, depth), f32),
        vmem((total, depth), bf16),
        vmem((shards - 1, rows, depth), bf16),
        vmem((total, depth), bf16),
        vmem((chunks, 2, quarter, width), f32),
        vmem((chunks, 2, quarter, width), f32),
        vmem((chunks, 2, quarter, width), f32),
        vmem((chunks, 2, quarter, width), bf16),
        vmem((chunks, 2, quarter, width), bf16),
        vmem((chunks, 4, 2, quarter, width), bf16),
        vmem((total, depth), bf16),
        vmem((shards - 1, rows, depth), bf16),
        vmem((2 * rows, depth), bf16),
        *[vmem((n, rows, piece), bf16) for n in (owners, ways, ways, owners)],
        *[vmem((n, rows, piece), f32) for n in (owners, ways, ways, owners)],
        vmem((1, depth), f32),
        vmem((shards - 1, 1, depth), f32),
        dma((SLOTS,)), dma((SLOTS,)), dma((chunks,)),
        *[dma((shards - 1,)) for _ in range(8)],
    ]
    for _ in range(2):
        scratch += [dma((chunks,)), dma((chunks,))]
        scratch += [dma((2, chunks)) for _ in range(6)]
    scratch += [dma((ways,)) for _ in range(8)] + [dma((shards - 1,)) for _ in range(2)]
    flops = 2 * total * depth * hidden * 8
    return pl.pallas_call(
        functools.partial(layer_kernel, dims),
        out_shape=(
            jax.ShapeDtypeStruct((rows, depth), f32),
            jax.ShapeDtypeStruct((1, depth), f32),
        ),
        in_specs=[pl.BlockSpec(memory_space=vmem)] * 4 + [pl.BlockSpec(memory_space=pl.ANY)] * 3,
        out_specs=(pl.BlockSpec(memory_space=vmem), pl.BlockSpec(memory_space=vmem)),
        scratch_shapes=scratch,
        compiler_params=pltpu.CompilerParams(
            collective_id=0, has_side_effects=True, vmem_limit_bytes=VMEM_LIMIT
        ),
        cost_estimate=pl.CostEstimate(
            flops=flops, bytes_accessed=10 * depth * hidden, transcendentals=0
        ),
    )(tokens, probe, signs, inner, gate_weight, up_weight, down_weight)


def on_device(tokens, probe, signs, gate_weight, up_weight, down_weight):
    index = jnp.arange(LANE, dtype=jnp.int32)
    parity = lax.population_count(index[:, None] & index[None, :]) & 1
    inner = jnp.where(parity == 0, 1.0, -1.0).astype(jnp.bfloat16)
    rotated_product, diagonal_estimate = layer(
        tokens, probe, signs[None, :], inner, gate_weight, up_weight, down_weight
    )
    return (rotated_product, diagonal_estimate[0])


def solution(mesh):
    placed = (
        P("tok", "ch"),
        P("tok", "ch"),
        P("ch"),
        P("ch", "tok"),
        P("ch", "tok"),
        P("tok", "ch"),
    )
    return jax.shard_map(
        on_device, mesh=mesh, in_specs=placed, out_specs=(P("tok", "ch"), P("ch")), check_vma=False
    )
```

```python
import functools
import math

import jax
import jax.numpy as jnp
from jax import lax
from jax.experimental import pallas as pl
from jax.experimental.pallas import tpu as pltpu
from jax.sharding import PartitionSpec as P

D = 16384
VMEM_LIMIT = 63 * 1024 * 1024


LANE = 128
SLOTS = 3
HOP = 2
NT = (((1,), (1,)), ((), ()))


class Pair:
    def __init__(self, *copies):
        self.copies = copies

    def start(self):
        for copy in self.copies:
            copy.start()

    def wait_recv(self):
        for copy in self.copies:
            copy.wait_recv()

    def wait_send(self):
        for copy in self.copies:
            copy.wait_send()


def butterfly(parts):
    span = 1
    while span < len(parts):
        for n in range(len(parts)):
            if n & span == 0:
                low, high = parts[n], parts[n + span]
                parts[n], parts[n + span] = low + high, low - high
        span *= 2
    return parts


def rotate_local(values, inner, precision):
    rows, lane = values.shape[0], inner.shape[0]
    groups = values.shape[1] // lane
    stacked = jnp.concatenate([values[:, g * lane : (g + 1) * lane] for g in range(groups)], axis=0)
    turned = jnp.dot(stacked, inner, precision=precision, preferred_element_type=jnp.float32)
    parts = butterfly([turned[g * rows : (g + 1) * rows] for g in range(groups)])
    return jnp.concatenate(parts, axis=1)


def layer_kernel(
    dims, tokens_in, probe, signs, inner, gate_hbm, up_hbm, down_hbm, out_ref, diag_ref, *scratch
):
    shards, rows, ways, chunks, width, owners = dims
    zs = ways // 2
    (
        x, gate_buf, up_buf, down_buf, sums, to_sib, from_sib, from_z, to_zt, from_zt, slope_up, active, hid,
        out_acc, o_send, o_recv, o_all, from_z2, grads,
        in_acc, k_recv, x_in, t_own, t_got, t_sum, t_res, f_own, f_got, f_sum, f_res,
        diag_own, diag_got,
        gate_sem, up_sem, down_sem, x_ss, x_rs, os_ss, os_rs, og_ss, og_rs, k_ss, k_rs,
        a_ss, a_rs, b_ss, b_rs, d_ss, d_rs, s_ss, s_rs,
        a2_ss, a2_rs, b2_ss, b2_rs, d2_ss, d2_rs, s2_ss, s2_rs,
        t1_ss, t1_rs, t2_ss, t2_rs, f1_ss, f1_rs, f2_ss, f2_rs, g_ss, g_rs, t_ss, t_rs,
    ) = scratch
    tok = lax.axis_index("tok")
    ch = lax.axis_index("ch")
    z, core = ch // 2, ch % 2
    per = shards // 4
    quarter = per * rows
    last = zs - 1
    f32, bf16 = jnp.float32, jnp.bfloat16

    def loads(f):
        slot = lax.rem(f, SLOTS)
        cols = pl.ds(pl.multiple_of(f * width, width), width)
        return (
            pltpu.make_async_copy(gate_hbm.at[:, cols], gate_buf.at[slot], gate_sem.at[slot]),
            pltpu.make_async_copy(up_hbm.at[:, cols], up_buf.at[slot], up_sem.at[slot]),
        )

    def load_down(f):
        at = pl.ds(pl.multiple_of(f * width, width), width)
        return pltpu.make_async_copy(down_hbm.at[at, :], down_buf.at[f], down_sem.at[f])

    def remote(src, dst, ss, rs, t, c):
        return pltpu.make_async_remote_copy(
            src_ref=src, dst_ref=dst, send_sem=ss, recv_sem=rs,
            device_id=(t, c), device_id_type=pl.DeviceIdType.MESH,
        )

    for f in range(SLOTS):
        for copy in loads(f):
            copy.start()

    sib = z * 2 + 1 - core
    barrier = pltpu.get_barrier_semaphore()

    def greet(t, c):
        pl.semaphore_signal(
            barrier, inc=1, device_id=(t, c), device_id_type=pl.DeviceIdType.MESH
        )

    for d in range(1, shards):
        greet(lax.rem(tok + d, shards), ch)
    for d in range(1, ways):
        greet(tok, lax.rem(ch + d, ways))
    pl.semaphore_wait(barrier, shards + ways - 2)

    def only(index, run):
        if owners == ways:
            run()
        else:
            pl.when(index < owners)(run)

    def across(own, got, summed, res, ss1, rs1, ss2, rs2):
        others = range(1, ways)
        to = {d: lax.rem(ch + d, ways) for d in others}
        of = {d: lax.rem(ch + ways - d, ways) for d in others}

        def out1(d):
            return remote(own.at[to[d]], got.at[ch], ss1.at[d], rs1.at[ch], tok, to[d])

        def in1(d):
            return remote(own.at[0], got.at[of[d]], ss1.at[d], rs1.at[of[d]], tok, of[d])

        def out2(d):
            return remote(summed.at[to[d]], res.at[ch], ss2.at[d], rs2.at[ch], tok, to[d])

        def in2(d):
            return remote(summed.at[0], res.at[of[d]], ss2.at[d], rs2.at[of[d]], tok, of[d])

        for d in others:
            only(to[d], lambda: out1(d).start())

        def combine():
            got[ch] = own[ch]
            for d in others:
                in1(d).wait_recv()
            parts = butterfly([got[n].astype(f32) for n in range(ways)])
            for n in range(ways):
                summed[n] = parts[n].astype(summed.dtype)
            for d in others:
                out2(d).start()
            res[ch] = summed[ch]

        only(ch, combine)
        for d in others:
            only(of[d], lambda: in2(d).wait_recv())
            only(to[d], lambda: out1(d).wait_send())
        only(ch, lambda: [out2(d).wait_send() for d in others] and None)

    root_scale = 1.0 / math.sqrt(D)
    piece = tokens_in.shape[1] // owners
    channel_signs = (2 * signs[...] - 1).astype(f32)
    probe_signs = (2 * probe[...] - 1).astype(f32)
    start = (probe_signs * channel_signs).astype(bf16)
    for n in range(owners):
        t_own[n] = start[:, n * piece : (n + 1) * piece]
    across(t_own, t_got, t_sum, t_res, t1_ss, t1_rs, t2_ss, t2_rs)
    start = jnp.concatenate([t_res[n] for n in range(owners)], axis=1)
    x_in[:rows] = tokens_in[...]
    x_in[rows:] = (rotate_local(start, inner[...], None) * root_scale).astype(bf16)

    def place(s):
        owner = s // per
        side = lax.rem(owner % 2 + core, 2)
        return (side * 2 + owner // 2) * per + s % per

    def peers(make):
        return [make(d, lax.rem(tok + d, shards)) for d in range(1, shards)]

    mine = pl.ds(pl.multiple_of(place(tok) * 2 * rows, 2 * rows), 2 * rows)
    x[mine, :] = x_in[...]
    gathers = peers(
        lambda d, p: remote(x_in, x.at[mine, :], x_ss.at[d - 1], x_rs.at[d - 1], p, ch)
    )
    for copy in gathers:
        copy.start()
    for copy in gathers:
        copy.wait()

    def ends():
        for e in range(2):
            far = last - z if e == 0 else z
            near = z if e == 0 else last - z
            toward = ch - 2 if e == 0 else ch + 2
            away = ch + 2 if e == 0 else ch - 2
            yield e, far, near, toward, away

    def in_range(f):
        return jnp.logical_and(f >= 0, f < chunks)

    def when(*conditions):
        return pl.when(functools.reduce(jnp.logical_and, conditions))

    def line(i, hop, chunk_at, part, add_sib, a_copy, recv, b_copy, finish, d_copy, s_copy):
        n1 = i - 1

        @pl.when(in_range(n1))
        def _():
            a_copy(chunk_at(n1)).wait_recv()
            add_sib(chunk_at(n1))

        for e, far, near, toward, away in ends():
            n2 = i - 1 - hop * far

            @pl.when(in_range(n2))
            def _():
                f = chunk_at(n2)

                @pl.when(far > 0)
                def _():
                    b_copy(e, f, toward).wait_recv()
                    recv(e, f)

                @pl.when(near > 0)
                def _():
                    part(e, f)
                    b_copy(e, f, toward).start()

                @pl.when(near == 0)
                def _():
                    finish(e, f)
                    d_copy(e, f, away).start()
                    s_copy(e, f).start()

            n3 = i - 1 - hop * last - near

            @when(in_range(n3), near > 0)
            def _():
                f = chunk_at(n3)
                d_copy(e, f, away).wait_recv()

                @pl.when(far > 0)
                def _():
                    d_copy(e, f, away).start()

                s_copy(e, f).start()

    def drain(a_copy, b_copy, d_copy, s_copy):
        def body(f, carry):
            a_copy(f).wait_send()
            for e, far, near, toward, away in ends():
                pl.when(near > 0)(lambda: b_copy(e, f, toward).wait_send())
                pl.when(far > 0)(lambda: d_copy(e, f, away).wait_send())
                s_copy(e, f).wait_send()
            return carry

        lax.fori_loop(0, chunks, body, 0)

    lag, lag2 = 2 + (1 + HOP) * last, 2 + 2 * last

    def block_of(e):
        return pl.ds(pl.multiple_of((e * 2 + core) * quarter, quarter), quarter)

    half = pl.ds(0, 2 * quarter)

    def a_copy(f):
        return remote(to_sib.at[f], from_sib.at[f], a_ss.at[f], a_rs.at[f], tok, sib)

    def b_copy(e, f, c):
        return Pair(
            remote(sums.at[f, e, :, 0], from_z.at[f, e], b_ss.at[e, f], b_rs.at[e, f], tok, c),
            remote(to_zt.at[f, e], from_zt.at[f, e], t_ss.at[e, f], t_rs.at[e, f], tok, c),
        )

    def d_copy(e, f, c):
        ref = hid.at[f, block_of(e), :]
        return remote(ref, ref, d_ss.at[e, f], d_rs.at[e, f], tok, c)

    def s_copy(e, f):
        ref = hid.at[f, block_of(e), :]
        return remote(ref, ref, s_ss.at[e, f], s_rs.at[e, f], tok, sib)

    def sib_recv(e, f):
        other = pl.ds(pl.multiple_of((e * 2 + 1 - core) * quarter, quarter), quarter)
        ref = hid.at[f, other, :]
        return remote(ref, ref, s_ss.at[e, f], s_rs.at[e, f], tok, sib)

    def add_sib(f):
        sums[f] += from_sib[f]

    def recv(e, f):
        sums[f, e, :, 0] += from_z[f, e]
        sums[f, e, :, 1] += from_zt[f, e].astype(f32)

    def part1(e, f):
        to_zt[f, e] = sums[f, e, :, 1].astype(bf16)

    def finish(e, f):
        for p in range(per):
            gate_pre = sums[f, e, p, 0, :, :width]
            up_pre = sums[f, e, p, 0, :, width:]
            gate_tan = sums[f, e, p, 1, :, :width]
            up_tan = sums[f, e, p, 1, :, width:]
            sig = jax.nn.sigmoid(gate_pre)
            act = gate_pre * sig
            slope = sig * (1.0 + gate_pre * (1.0 - sig))
            su = slope * up_pre
            slope_up[f, p * rows : (p + 1) * rows, :] = su
            active[f, p * rows : (p + 1) * rows, :] = act
            at = (e * 2 + core) * quarter + p * rows
            hid[f, pl.ds(pl.multiple_of(at, rows), rows), :] = (
                su * gate_tan + act * up_tan
            ).astype(bf16)

    out_acc[...] = jnp.zeros_like(out_acc)

    def forward(i, carry):
        @pl.when(i < chunks)
        def _():
            load_down(i).start()
            for copy in loads(i):
                copy.wait()
            slot = lax.rem(i, SLOTS)
            for n, buf in enumerate((gate_buf, up_buf)):
                part = jnp.dot(x[...], buf[slot], preferred_element_type=f32)
                cols = slice(n * width, (n + 1) * width)
                part = part.reshape(4, per, 2, rows, width)
                for e in range(2):
                    sums[i, e, :, :, :, cols] = part[e]
                    to_sib[i, e, :, :, :, cols] = part[2 + e]
            a_copy(i).start()

            @pl.when(i + SLOTS < chunks)
            def _():
                for copy in loads(i + SLOTS):
                    copy.start()

        line(
            i, HOP, lambda n: n, part1, add_sib, a_copy, recv, b_copy, finish,
            d_copy, s_copy,
        )
        n4 = i - lag

        @pl.when(n4 >= 0)
        def _():
            for e in range(2):
                sib_recv(e, n4).wait_recv()
            load_down(n4).wait()
            out_acc[...] += jnp.dot(hid[n4], down_buf[n4], preferred_element_type=f32)

        return carry

    lax.fori_loop(0, chunks + lag, forward, 0)
    drain(a_copy, b_copy, d_copy, s_copy)

    def scatter(acc, send, recv, ss, rs):
        send[...] = acc[...].astype(bf16)

        def make(d, p):
            at = pl.ds(pl.multiple_of(p * rows, rows), rows)
            return remote(send.at[at, :], recv.at[d - 1], ss.at[d - 1], rs.at[d - 1], p, ch)

        copies = peers(make)
        for copy in copies:
            copy.start()
        total = acc[pl.ds(pl.multiple_of(tok * rows, rows), rows), :]
        for d, copy in enumerate(copies):
            copy.wait()
            total = total + recv[d].astype(f32)
        return total

    here = pl.ds(pl.multiple_of(place(tok) * rows, rows), rows)
    o_all[here, :] = scatter(out_acc, o_send, o_recv, os_ss, os_rs).astype(bf16)
    gathers = peers(
        lambda d, p: remote(
            o_all.at[here, :], o_all.at[here, :], og_ss.at[d - 1], og_rs.at[d - 1], p, ch
        )
    )
    for copy in gathers:
        copy.start()
    for d, copy in enumerate(gathers):
        copy.wait()

    def a2_copy(f):
        at = (f, slice(None), slice(None), 0, slice(None), pl.ds(0, width))
        return remote(to_sib.at[at], from_sib.at[at], a2_ss.at[f], a2_rs.at[f], tok, sib)

    def b2_copy(e, f, c):
        src = sums.at[f, e, :, 0, :, pl.ds(0, width)]
        return remote(
            src, from_z2.at[f, e], b2_ss.at[e, f], b2_rs.at[e, f], tok, c
        )

    def d2_copy(e, f, c):
        ref = grads.at[f, e * 2 + core]
        return remote(ref, ref, d2_ss.at[e, f], d2_rs.at[e, f], tok, c)

    def s2_copy(e, f):
        ref = grads.at[f, e * 2 + core]
        return remote(ref, ref, s2_ss.at[e, f], s2_rs.at[e, f], tok, sib)

    def sib2_recv(e, f):
        ref = grads.at[f, e * 2 + 1 - core]
        return remote(ref, ref, s2_ss.at[e, f], s2_rs.at[e, f], tok, sib)

    def add_sib2(f):
        sums[f, :, :, 0, :, :width] += from_sib[f, :, :, 0, :, :width]

    def recv2(e, f):
        sums[f, e, :, 0, :, :width] += from_z2[f, e]

    def finish2(e, f):
        back = sums[f, e, :, 0, :, :width].reshape(quarter, width)
        grads[f, e * 2 + core, 0] = (back * slope_up[f]).astype(bf16)
        grads[f, e * 2 + core, 1] = (back * active[f]).astype(bf16)

    def chunk_at(n):
        return chunks - 1 - n

    in_acc[...] = jnp.zeros_like(in_acc)

    def backward(i, carry):
        @pl.when(i < chunks)
        def _():
            f = chunk_at(i)
            part = lax.dot_general(down_buf[f], o_all[...], NT, preferred_element_type=f32).T
            part = part.reshape(4, per, rows, width)
            for e in range(2):
                sums[f, e, :, 0, :, :width] = part[e]
                to_sib[f, e, :, 0, :, :width] = part[2 + e]
            a2_copy(f).start()

        line(
            i, 1, chunk_at, lambda e, f: None, add_sib2, a2_copy, recv2, b2_copy, finish2, d2_copy, s2_copy
        )
        n4 = i - lag2

        @pl.when(n4 >= 0)
        def _():
            f = chunk_at(n4)
            for e in range(2):
                sib2_recv(e, f).wait_recv()

            @pl.when(f + SLOTS < chunks)
            def _():
                for copy in loads(f):
                    copy.wait()

            slot = lax.rem(f, SLOTS)
            both = grads[f]
            for n, buf in enumerate((gate_buf, up_buf)):
                piece = both[:, n].reshape(4 * quarter, width)
                in_acc[...] += lax.dot_general(buf[slot], piece, NT, preferred_element_type=f32)

            @pl.when(f >= SLOTS)
            def _():
                for copy in loads(f - SLOTS):
                    copy.start()

        return carry

    lax.fori_loop(0, chunks + lag2, backward, 0)
    drain(a2_copy, b2_copy, d2_copy, s2_copy)
    out_acc[...] = in_acc[...].T
    back_tokens = scatter(out_acc, o_send, k_recv, k_ss, k_rs)
    turned = rotate_local(back_tokens, inner[...].astype(f32), lax.Precision.HIGHEST)
    for n in range(owners):
        f_own[n] = turned[:, n * piece : (n + 1) * piece]
    across(f_own, f_got, f_sum, f_res, f1_ss, f1_rs, f2_ss, f2_rs)
    turned = jnp.concatenate([f_res[n] for n in range(owners)], axis=1)
    product = turned * root_scale * channel_signs
    out_ref[...] = product
    diag_own[...] = jnp.sum(probe_signs * product, axis=0, keepdims=True)
    copies = peers(
        lambda d, p: remote(diag_own, diag_got.at[d - 1], g_ss.at[d - 1], g_rs.at[d - 1], p, ch)
    )
    for copy in copies:
        copy.start()
    diagonal = diag_own[...]
    for d, copy in enumerate(copies):
        copy.wait()
        diagonal = diagonal + diag_got[d]
    diag_ref[...] = diagonal / (shards * rows)


def layer(tokens, probe, signs, inner, gate_weight, up_weight, down_weight):
    shards, ways = lax.axis_size("tok"), lax.axis_size("ch")
    rows, depth = tokens.shape
    hidden = gate_weight.shape[1]
    width = max(w for w in range(128, 513, 128) if hidden % w == 0)
    chunks = hidden // width
    total, quarter = shards * rows, shards * rows // 4
    owners = min(ways, depth // LANE)
    piece = depth // owners
    per = shards // 4
    dims = (shards, rows, ways, chunks, width, owners)
    f32, bf16, vmem = jnp.float32, jnp.bfloat16, pltpu.VMEM
    dma = pltpu.SemaphoreType.DMA
    scratch = [
        vmem((2 * total, depth), bf16),
        vmem((SLOTS, depth, width), bf16),
        vmem((SLOTS, depth, width), bf16),
        vmem((chunks, width, depth), bf16),
        *[vmem((chunks, 2, per, 2, rows, 2 * width), f32) for _ in range(3)],
        *[vmem((chunks, 2, per, rows, 2 * width), kind) for kind in (f32, bf16, bf16)],
        vmem((chunks, quarter, width), f32),
        vmem((chunks, quarter, width), f32),
        vmem((chunks, total, width), bf16),
        vmem((total, depth), f32),
        vmem((total, depth), bf16),
        vmem((shards - 1, rows, depth), bf16),
        vmem((total, depth), bf16),
        vmem((chunks, 2, per, rows, width), f32),
        vmem((chunks, 4, 2, quarter, width), bf16),
        vmem((depth, total), f32),
        vmem((shards - 1, rows, depth), bf16),
        vmem((2 * rows, depth), bf16),
        *[vmem((n, rows, piece), bf16) for n in (owners, ways, ways, owners)],
        *[vmem((n, rows, piece), f32) for n in (owners, ways, ways, owners)],
        vmem((1, depth), f32),
        vmem((shards - 1, 1, depth), f32),
        dma((SLOTS,)), dma((SLOTS,)), dma((chunks,)),
        *[dma((shards - 1,)) for _ in range(8)],
    ]
    for _ in range(2):
        scratch += [dma((chunks,)), dma((chunks,))]
        scratch += [dma((2, chunks)) for _ in range(6)]
    scratch += [dma((ways,)) for _ in range(8)] + [dma((shards - 1,)) for _ in range(2)]
    scratch += [dma((2, chunks)), dma((2, chunks))]
    flops = 2 * total * depth * hidden * 8
    return pl.pallas_call(
        functools.partial(layer_kernel, dims),
        out_shape=(
            jax.ShapeDtypeStruct((rows, depth), f32),
            jax.ShapeDtypeStruct((1, depth), f32),
        ),
        in_specs=[pl.BlockSpec(memory_space=vmem)] * 4 + [pl.BlockSpec(memory_space=pl.ANY)] * 3,
        out_specs=(pl.BlockSpec(memory_space=vmem), pl.BlockSpec(memory_space=vmem)),
        scratch_shapes=scratch,
        compiler_params=pltpu.CompilerParams(
            collective_id=0, has_side_effects=True, vmem_limit_bytes=VMEM_LIMIT
        ),
        cost_estimate=pl.CostEstimate(
            flops=flops, bytes_accessed=10 * depth * hidden, transcendentals=0
        ),
    )(tokens, probe, signs, inner, gate_weight, up_weight, down_weight)


def on_device(tokens, probe, signs, gate_weight, up_weight, down_weight):
    index = jnp.arange(LANE, dtype=jnp.int32)
    parity = lax.population_count(index[:, None] & index[None, :]) & 1
    inner = jnp.where(parity == 0, 1.0, -1.0).astype(jnp.bfloat16)
    rotated_product, diagonal_estimate = layer(
        tokens, probe, signs[None, :], inner, gate_weight, up_weight, down_weight
    )
    return (rotated_product, diagonal_estimate[0])


def solution(mesh):
    placed = (
        P("tok", "ch"),
        P("tok", "ch"),
        P("ch"),
        P("ch", "tok"),
        P("ch", "tok"),
        P("tok", "ch"),
    )
    return jax.shard_map(
        on_device, mesh=mesh, in_specs=placed, out_specs=(P("tok", "ch"), P("ch")), check_vma=False
    )
```
